32 devices in a mesh: seq: 8 (over z, x), head: 4 (over y, core).
Axes of the slice: x: 2, y: 2, z: 4, core: 2. Of those that a mesh axis runs over, the one named last changes fastest.
Arguments:
- tokens: bfloat16 [8192, 4096], P('seq'), may hold values from -6 to 6
- w_query: bfloat16 [4096, 4096], P(None, 'head'), may hold values from -0.09375 to 0.09375
- w_key: bfloat16 [4096, 4096], P(None, 'head'), may hold values from -0.09375 to 0.09375
- w_value: bfloat16 [4096, 4096], P(None, 'head'), may hold values from -0.09375 to 0.09375
- norm_gain: float32 [4096], P('head'), may hold values from 0.25 to 1.75
- w_out: bfloat16 [4096, 4096], P('head'), may hold values from -0.125 to 0.125
Outputs:
- mixed: bfloat16 [8192, 4096], P('seq', 'head')
The draws below stay inside these ranges and needn't reach their ends.
All inputs are finite; a program needn't handle non-finite values.
Results may differ from the reference program's by a relative error of at most 0.02.
Values may be sent and summed in bfloat16 or wider, within the bound.
A program may use at most 128 MiB of HBM per device.

```python
import jax
import jax.numpy as jnp
from jax import lax

D = 4096
HEADS = 32
HEAD_DIM = 128
SPAN = 128
TOKENS = 8192
N_HEAD = 4


def spiked(result, rng, source, target, shards_of, factor):
    owner, partner = [(jnp.arange(result.shape[position]) // (result.shape[position] // shards_of)).reshape([-1 if axis == position else 1 for axis in range(result.ndim)]) for position in (source, target)]
    chosen = jax.random.permutation(rng, shards_of)[partner]
    strong = (owner == chosen) | (owner == (partner + shards_of // 2) % shards_of)
    return jnp.where(strong, factor * result, result)


def level_of(key, extent, split, least, top_value):
    loudness = 1.0
    for axis_at, blocks in split:
        draws = jax.random.uniform(jax.random.fold_in(jax.random.fold_in(key, 6), axis_at), (blocks,), jnp.float32, least / len(split), top_value / len(split))
        loudness = loudness * jnp.repeat(jnp.exp(draws), extent[axis_at] // blocks).reshape((-1,) + (1,) * (len(extent) - 1 - axis_at))
    return loudness


def noise(key, shape, scale, limit, cuts=(), held_as=jnp.bfloat16):
    result = scale * jax.random.normal(key, shape, jnp.float32)
    if cuts:
        result = result * level_of(key, shape, cuts, -0.22, 0.18)
    return jnp.clip(result, -limit, limit).astype(held_as)


def bell_draw_with(rng, extent, scale, bound, cuts, heavy, kind=jnp.bfloat16):
    array = scale * jax.random.normal(rng, extent, jnp.float32)
    if cuts:
        array = array * level_of(rng, extent, cuts, -0.22, 0.18)
    return jnp.clip(spiked(array, jax.random.fold_in(rng, 3), *heavy), -bound, bound).astype(kind)


def setup_inputs(seed: int = 0) -> dict:
    keys = jax.random.split(jax.random.key(seed), 7)
    return {
        "tokens": noise(keys[0], (TOKENS, D), 1.0, 6.0, ((0, 8),)),
        "w_query": noise(keys[1], (D, D), D ** -0.5, 0.09375, ((1, 4),)),
        "w_key": noise(keys[2], (D, D), D ** -0.5, 0.09375, ((1, 4),)),
        "w_value": noise(keys[3], (D, D), D ** -0.5, 0.09375, ((1, 4),)),
        "norm_gain": jnp.clip(1.0 + 0.15 * jax.random.normal(keys[4], (D,), jnp.float32), 0.25, 1.75),
        "w_out": bell_draw_with(keys[5], (D, D), D ** -0.5, 0.125, ((0, 4),), (0, 1, 4, 2.0)),
    }


def lower_mask(size):
    rows = lax.broadcasted_iota(jnp.int32, (size, size), 0)
    cols = lax.broadcasted_iota(jnp.int32, (size, size), 1)
    return (rows >= cols).astype(jnp.float32)

def reference(tokens, w_query, w_key, w_value, norm_gain, w_out):
    count = tokens.shape[0]
    blocks = count // SPAN
    shape4 = (blocks, SPAN, HEADS, HEAD_DIM)
    q_rows = jnp.dot(tokens, w_query, preferred_element_type=jnp.float32).astype(jnp.bfloat16).reshape(shape4)
    k_rows = jnp.dot(tokens, w_key, preferred_element_type=jnp.float32).astype(jnp.bfloat16).reshape(shape4)
    v_rows = jnp.dot(tokens, w_value, preferred_element_type=jnp.float32).astype(jnp.bfloat16).reshape(shape4)
    masking = lower_mask(SPAN)

    def advance(state, pieces):
        q_blk, k_blk, v_blk = pieces
        q_f = q_blk.astype(jnp.float32)
        k_f = k_blk.astype(jnp.float32)
        v_f = v_blk.astype(jnp.float32)
        scores = (jnp.einsum('ihd,jhd->hij', q_f, k_f) * masking).astype(jnp.bfloat16)
        within = jnp.einsum('hij,jhe->ihe', scores.astype(jnp.float32), v_f)
        prior = state.astype(jnp.bfloat16).astype(jnp.float32)
        across = jnp.einsum('ihd,hde->ihe', q_f, prior)
        new_state = state + jnp.einsum('jhd,jhe->hde', k_f, v_f)
        return (new_state, within + across)
    start_state = jnp.zeros((HEADS, HEAD_DIM, HEAD_DIM), jnp.float32)
    final_state, raw = lax.scan(advance, start_state, (q_rows, k_rows, v_rows))
    power = lax.optimization_barrier(jnp.mean(raw * raw, axis=-1, keepdims=True))
    normed = raw * lax.rsqrt(power + 1e-06) * norm_gain.reshape(HEADS, HEAD_DIM)
    attended = normed.astype(jnp.bfloat16).reshape(count, D)
    group_width = D // N_HEAD
    grouped = attended.reshape(count, N_HEAD, group_width).transpose(1, 0, 2)
    out_rows = w_out.reshape(N_HEAD, group_width, D)

    def add_group(total, pieces):
        left, right = pieces
        partial_sum = jnp.dot(left, right, preferred_element_type=jnp.float32).astype(jnp.bfloat16)
        partial_sum = lax.optimization_barrier(partial_sum)
        return (total + partial_sum.astype(jnp.float32), None)
    summed, unused = lax.scan(add_group, jnp.zeros((count, D), jnp.float32), (grouped, out_rows))
    return summed.astype(jnp.bfloat16)
```

```python
import functools

import jax
import jax.numpy as jnp
from jax import lax
from jax.experimental import pallas as pl
from jax.experimental.pallas import tpu as pltpu
from jax.sharding import PartitionSpec as P

HEAD_DIM = 128
CHUNK = 256
PAIR = 2 * HEAD_DIM
ROWS = 512
AHEAD = 2
MESH = pl.DeviceIdType.MESH
BF16 = jnp.bfloat16
F32 = jnp.float32


def kernel(
    n_seq, n_head,
    tok_hbm, wq_hbm, wk_hbm, wv_hbm, gain_ref, wo_hbm, out_hbm,
    tok, kbuf, vbuf, wq, wo, q, k, v, att, pre, total, carried,
    scan_out, scan_in, sib_out, sib_in, y_out, y_in, own, obuf,
    tok_sem, k_sem, v_sem, wq_sem, wo_sem, o_sem,
    scan_ss, scan_rs, sib_ss, sib_rs, y_ss, y_rs,
):
    count, depth = tok.shape
    width = q.shape[1]
    heads = width // HEAD_DIM
    pairs = width // PAIR
    cols = wo.shape[1] // n_head
    nt = count // CHUNK
    ny = n_head // 2
    rounds = (n_seq - 1).bit_length()
    s = lax.axis_index("seq")
    h = lax.axis_index("head")
    y, c = h // 2, h % 2
    sib = y * 2 + 1 - c

    def tok_copy(t):
        rows = pl.ds(pl.multiple_of(t * CHUNK, CHUNK), CHUNK)
        return pltpu.make_async_copy(tok_hbm.at[rows], tok.at[rows], tok_sem.at[t])

    def panel(src, dst, sem, p):
        return pltpu.make_async_copy(
            src.at[:, pl.ds(p * PAIR, PAIR)], dst.at[p % 2], sem.at[p % 2]
        )

    wq_copy = pltpu.make_async_copy(wq_hbm, wq, wq_sem)
    wo_copy = pltpu.make_async_copy(wo_hbm, wo, wo_sem)

    panel(wk_hbm, kbuf, k_sem, 0).start()
    for t in range(nt):
        tok_copy(t).start()
    panel(wv_hbm, vbuf, v_sem, 0).start()

    barrier = pltpu.get_barrier_semaphore()
    expected = jnp.int32(ny)
    pl.semaphore_signal(barrier, inc=1, device_id=(s, sib), device_id_type=MESH)
    for j in range(1, ny):
        peer = lax.rem(y + j, ny) * 2 + c
        pl.semaphore_signal(barrier, inc=1, device_id=(s, peer), device_id_type=MESH)
    for r in range(rounds):
        d = 1 << r

        @pl.when(s + d < n_seq)
        def _():
            pl.semaphore_signal(barrier, inc=1, device_id=(s + d, h), device_id_type=MESH)

        @pl.when(s >= d)
        def _():
            pl.semaphore_signal(barrier, inc=1, device_id=(s - d, h), device_id_type=MESH)

        expected += (s + d < n_seq).astype(jnp.int32) + (s >= d).astype(jnp.int32)
    pl.semaphore_wait(barrier, expected)

    def scan_copy(p, r):
        return pltpu.make_async_remote_copy(
            src_ref=scan_out.at[p, r], dst_ref=scan_in.at[p, r],
            send_sem=scan_ss.at[p, r], recv_sem=scan_rs.at[p, r],
            device_id=(lax.rem(s + (1 << r), n_seq), h), device_id_type=MESH,
        )

    def scan_send(p, r):
        @pl.when(s + (1 << r) < n_seq)
        def _():
            scan_out[p, r] = (carried[2 * p:2 * p + 2] + total[2 * p:2 * p + 2]).astype(BF16)
            scan_copy(p, r).start()

    def scan_recv(p, r):
        @pl.when(s >= (1 << r))
        def _():
            scan_copy(p, r).wait_recv()
            carried[2 * p:2 * p + 2] += scan_in[p, r].astype(F32)

    stage = [0] * pairs

    def scan_step(done):
        for p in range(done):
            r = stage[p]
            if r > rounds:
                continue
            if r > 0:
                scan_recv(p, r - 1)
            if r < rounds:
                scan_send(p, r)
            stage[p] = r + 1

    carried[...] = jnp.zeros_like(carried)

    def project(w, dst, p, wait):
        @pl.loop(0, count // ROWS)
        def _(i):
            if wait:
                for j in range(ROWS // CHUNK):
                    tok_copy(i * (ROWS // CHUNK) + j).wait()
            rows = pl.ds(pl.multiple_of(i * ROWS, ROWS), ROWS)
            dst[rows, p * PAIR:(p + 1) * PAIR] = jnp.dot(
                tok[rows, :], w[...], preferred_element_type=F32
            ).astype(BF16)

    for p in range(pairs):
        panel(wk_hbm, kbuf, k_sem, p).wait()
        if p + 1 < pairs:
            panel(wk_hbm, kbuf, k_sem, p + 1).start()
            panel(wv_hbm, vbuf, v_sem, p + 1).start()
        if p == min(1, pairs - 1):
            wq_copy.start()
            wo_copy.start()
        project(kbuf.at[p % 2], k, p, p == 0)
        if p > 0:
            scan_step(p)
        panel(wv_hbm, vbuf, v_sem, p).wait()
        project(vbuf.at[p % 2], v, p, False)
        for e in range(2):
            hd = 2 * p + e
            lanes = slice(hd * HEAD_DIM, (hd + 1) * HEAD_DIM)
            run = jnp.zeros((HEAD_DIM, HEAD_DIM), F32)
            for t in range(nt):
                pre[t, hd] = run
                run = run + lax.dot_general(
                    k[t * CHUNK:(t + 1) * CHUNK, lanes], v[t * CHUNK:(t + 1) * CHUNK, lanes],
                    (((0,), (0,)), ((), ())), preferred_element_type=F32,
                )
            total[hd] = run
        scan_step(p + 1)

    def project_q(t):
        rows = pl.ds(pl.multiple_of(t * CHUNK, CHUNK), CHUNK)

        @pl.loop(0, pairs)
        def _(i):
            lanes = pl.ds(pl.multiple_of(i * PAIR, PAIR), PAIR)
            q[rows, lanes] = jnp.dot(
                tok[rows, :], wq[:, lanes], preferred_element_type=F32
            ).astype(BF16)

    wq_copy.wait()
    for t in range(AHEAD):
        project_q(t)
        scan_step(pairs)
    while min(stage) <= rounds:
        scan_step(pairs)
    wo_copy.wait()

    def sib_copy(t, j):
        return pltpu.make_async_remote_copy(
            src_ref=sib_out.at[t % 2, j], dst_ref=sib_in.at[t, j],
            send_sem=sib_ss.at[t, j], recv_sem=sib_rs.at[t, j],
            device_id=(s, sib), device_id_type=MESH,
        )

    def y_copy(t, j):
        return pltpu.make_async_remote_copy(
            src_ref=y_out.at[t, j - 1], dst_ref=y_in.at[t, j - 1],
            send_sem=y_ss.at[t, j - 1], recv_sem=y_rs.at[t, j - 1],
            device_id=(s, lax.rem(y + j, ny) * 2 + c), device_id_type=MESH,
        )

    def partial(dest):
        lanes = pl.ds(pl.multiple_of(dest * cols, cols), cols)
        return jnp.dot(att[...], wo[:, lanes], preferred_element_type=F32)

    order = list(range(1, ny)) + [0]

    @pl.loop(0, nt)
    def _(t):
        rows = pl.ds(pl.multiple_of(t * CHUNK, CHUNK), CHUNK)
        keep = lax.broadcasted_iota(jnp.int32, (CHUNK, CHUNK), 0) >= lax.broadcasted_iota(
            jnp.int32, (CHUNK, CHUNK), 1
        )
        for hd in range(heads):
            lanes = slice(hd * HEAD_DIM, (hd + 1) * HEAD_DIM)
            qh, kh, vh = q[rows, lanes], k[rows, lanes], v[rows, lanes]
            scores = lax.dot_general(
                qh, kh, (((1,), (1,)), ((), ())), preferred_element_type=F32
            )
            scores = jnp.where(keep, scores, 0.0).astype(BF16)
            prior = (carried[hd] + pre[t, hd]).astype(BF16)
            raw = jnp.dot(scores, vh, preferred_element_type=F32) + jnp.dot(
                qh, prior, preferred_element_type=F32
            )
            power = jnp.mean(raw * raw, axis=-1, keepdims=True)
            att[:, lanes] = (raw * lax.rsqrt(power + 1e-6) * gain_ref[:, lanes]).astype(BF16)

        @pl.when(t >= 2)
        def _():
            for j in range(ny):
                sib_copy(t - 2, j).wait_send()

        for j in order:
            sib_out[t % 2, j] = partial(lax.rem(y + j, ny) * 2 + 1 - c).astype(BF16)
            sib_copy(t, j).start()
        own[rows, :] = partial(h)
        for j in range(1, ny):
            mine = partial(lax.rem(y + j, ny) * 2 + c)
            sib_copy(t, j).wait_recv()
            y_out[t, j - 1] = (mine + sib_in[t, j].astype(F32)).astype(BF16)
            y_copy(t, j).start()
        sib_copy(t, 0).wait_recv()
        own[rows, :] += sib_in[t, 0].astype(F32)

        @pl.when(t + AHEAD < nt)
        def _():
            project_q(t + AHEAD)

    def out_copy(t):
        rows = pl.ds(t * CHUNK, CHUNK)
        return pltpu.make_async_copy(obuf.at[t % 2], out_hbm.at[rows], o_sem.at[t % 2])

    for t in range(nt):
        if t >= 2:
            out_copy(t - 2).wait()
        result = own[t * CHUNK:(t + 1) * CHUNK, :]
        for j in range(1, ny):
            y_copy(t, j).wait_recv()
            result = result + y_in[t, j - 1].astype(F32)
        obuf[t % 2] = result.astype(BF16)
        out_copy(t).start()
    for t in range(max(nt - 2, 0), nt):
        out_copy(t).wait()
        for j in range(ny):
            sib_copy(t, j).wait_send()
    for t in range(nt):
        for j in range(1, ny):
            y_copy(t, j).wait_send()
    for p in range(pairs):
        for r in range(rounds):
            @pl.when(s + (1 << r) < n_seq)
            def _():
                scan_copy(p, r).wait_send()


def local(n_seq, n_head, tokens, w_query, w_key, w_value, norm_gain, w_out):
    count, depth = tokens.shape
    width = w_query.shape[1]
    heads, pairs = width // HEAD_DIM, width // PAIR
    features = w_out.shape[1]
    cols = features // n_head
    nt, ny = count // CHUNK, n_head // 2
    rounds = (n_seq - 1).bit_length()
    dma = pltpu.SemaphoreType.DMA
    hbm = pl.BlockSpec(memory_space=pl.ANY)
    vmem = pl.BlockSpec(memory_space=pltpu.VMEM)
    return pl.pallas_call(
        functools.partial(kernel, n_seq, n_head),
        out_shape=jax.ShapeDtypeStruct((count, cols), BF16),
        in_specs=[hbm, hbm, hbm, hbm, vmem, hbm],
        out_specs=hbm,
        scratch_shapes=[
            pltpu.VMEM((count, depth), BF16),
            pltpu.VMEM((2, depth, PAIR), BF16),
            pltpu.VMEM((2, depth, PAIR), BF16),
            pltpu.VMEM((depth, width), BF16),
            pltpu.VMEM((width, features), BF16),
            pltpu.VMEM((count, width), BF16),
            pltpu.VMEM((count, width), BF16),
            pltpu.VMEM((count, width), BF16),
            pltpu.VMEM((CHUNK, width), BF16),
            pltpu.VMEM((nt, heads, HEAD_DIM, HEAD_DIM), F32),
            pltpu.VMEM((heads, HEAD_DIM, HEAD_DIM), F32),
            pltpu.VMEM((heads, HEAD_DIM, HEAD_DIM), F32),
            pltpu.VMEM((pairs, rounds, 2, HEAD_DIM, HEAD_DIM), BF16),
            pltpu.VMEM((pairs, rounds, 2, HEAD_DIM, HEAD_DIM), BF16),
            pltpu.VMEM((2, ny, CHUNK, cols), BF16),
            pltpu.VMEM((nt, ny, CHUNK, cols), BF16),
            pltpu.VMEM((nt, ny - 1, CHUNK, cols), BF16),
            pltpu.VMEM((nt, ny - 1, CHUNK, cols), BF16),
            pltpu.VMEM((count, cols), F32),
            pltpu.VMEM((2, CHUNK, cols), BF16),
            dma((nt,)), dma((2,)), dma((2,)), dma, dma, dma((2,)),
            dma((pairs, rounds)), dma((pairs, rounds)),
            dma((nt, ny)), dma((nt, ny)),
            dma((nt, ny - 1)), dma((nt, ny - 1)),
        ],
        compiler_params=pltpu.CompilerParams(
            collective_id=0, has_side_effects=True, vmem_limit_bytes=63 * 2**20
        ),
    )(tokens, w_query, w_key, w_value, norm_gain.reshape(1, width), w_out)


def solution(mesh):
    n_seq, n_head = mesh.shape["seq"], mesh.shape["head"]
    in_specs = (
        P("seq", None), P(None, "head"), P(None, "head"), P(None, "head"),
        P("head"), P("head", None),
    )
    return jax.shard_map(
        functools.partial(local, n_seq, n_head), mesh=mesh, in_specs=in_specs,
        out_specs=P("seq", "head"), check_vma=False,
    )
```

```python
import functools

import jax
import jax.numpy as jnp
from jax import lax
from jax.experimental import pallas as pl
from jax.experimental.pallas import tpu as pltpu
from jax.sharding import PartitionSpec as P

HEAD_DIM = 128
CHUNK = 256
PAIR = 2 * HEAD_DIM
ROWS = 512
MESH = pl.DeviceIdType.MESH
BF16 = jnp.bfloat16
F32 = jnp.float32


def kernel(
    n_seq, n_head, nx,
    tok_hbm, wq_hbm, wk_hbm, wv_hbm, gain_ref, wo_hbm, out_hbm,
    tok, kbuf, vbuf, qbuf, q, k, v, att, wcol, acc, pre, total, carried, group,
    x_out, x_in, z_out, z_in, obuf,
    tok_sem, k_sem, v_sem, q_sem, own_sem, o_sem,
    x_ss, x_rs, z_ss, z_rs, ws_ss, ws_rs, wx_ss, wx_rs, wf_ss, wf_rs,
    as_ss, as_rs, ay_ss, ay_rs, af_ss, af_rs,
):
    count, depth = tok.shape
    width = q.shape[1]
    heads = width // HEAD_DIM
    pairs = width // PAIR
    cols = acc.shape[1]
    nt = count // CHUNK
    nu = count // ROWS
    ny = n_head // 2
    nz = n_seq // nx
    share = width // 4
    s = lax.axis_index("seq")
    h = lax.axis_index("head")
    y, c = h // 2, h % 2
    z, x = s // nx, s % nx
    sib = y * 2 + 1 - c
    g = (z % 2) * 2 + x % 2
    flip_x = 1 - 2 * (x % 2)
    flip_z = nx * (1 - 2 * (z % 2))
    quad = [s + flip_x, s + flip_z, s + flip_x + flip_z]

    def remote(src, dst, ss, rs, dev):
        return pltpu.make_async_remote_copy(
            src_ref=src, dst_ref=dst, send_sem=ss, recv_sem=rs,
            device_id=dev, device_id_type=MESH,
        )

    def tok_copy(t):
        rows = pl.ds(pl.multiple_of(t * CHUNK, CHUNK), CHUNK)
        return pltpu.make_async_copy(tok_hbm.at[rows], tok.at[rows], tok_sem.at[t])

    def panel(src, dst, sem, p):
        return pltpu.make_async_copy(
            src.at[:, pl.ds(p * PAIR, PAIR)], dst.at[p % 2], sem.at[p % 2]
        )

    panel(wk_hbm, kbuf, k_sem, 0).start()
    for t in range(nt):
        tok_copy(t).start()
    panel(wv_hbm, vbuf, v_sem, 0).start()

    barrier = pltpu.get_barrier_semaphore()

    def greet(*dev):
        pl.semaphore_signal(barrier, inc=1, device_id=dev, device_id_type=MESH)

    for j in range(1, n_head):
        greet(s, lax.rem(h + j, n_head))
    for j in range(1, nx):
        greet(z * nx + lax.rem(x + j, nx), h)

    @pl.when(z > 0)
    def _():
        greet(s - nx, h)

    @pl.when(z < nz - 1)
    def _():
        greet(s + nx, h)

    greet(quad[2], h)
    pl.semaphore_wait(
        barrier,
        n_head + nx - 1 + (z > 0).astype(jnp.int32) + (z < nz - 1).astype(jnp.int32),
    )

    def block(head):
        return pl.ds(pl.multiple_of(head * cols, cols), cols)

    def rows_of(part):
        return pl.ds(pl.multiple_of(part * share, share), share)

    own_copy = pltpu.make_async_copy(wo_hbm.at[:, block(h)], wcol.at[h], own_sem)

    def ws_copy():
        return remote(wo_hbm.at[:, block(sib)], wcol.at[h], ws_ss, ws_rs, (s, sib))

    def ws_wait():
        remote(wo_hbm.at[:, block(h)], wcol.at[sib], ws_ss, ws_rs, (s, sib)).wait_recv()

    def wx_copy(j, e):
        dest = lax.rem(y + j, ny) * 2 + e
        return remote(
            wo_hbm.at[rows_of(g), block(dest)], wcol.at[h, rows_of(g)],
            wx_ss.at[j - 1, e], wx_rs.at[j - 1, c], (s, dest),
        )

    def source(j, e):
        return lax.rem(y - j + ny, ny) * 2 + e

    def wx_wait(j, e):
        hs = source(j, e)
        remote(
            wo_hbm.at[rows_of(g), block(h)], wcol.at[hs, rows_of(g)],
            wx_ss.at[j - 1, e], wx_rs.at[j - 1, e], (s, hs),
        ).wait_recv()

    def wf_copy(j, e, f):
        part = wcol.at[source(j, e), rows_of(g)]
        return remote(part, part, wf_ss.at[j - 1, e, f], wf_rs.at[j - 1, e, f], (quad[f], h))

    def wf_wait(j, e, f):
        gx, gz = g % 2, g // 2
        other = [gz * 2 + 1 - gx, (1 - gz) * 2 + gx, 3 - g][f]
        part = wcol.at[source(j, e), rows_of(other)]
        remote(
            part, part, wf_ss.at[j - 1, e, f], wf_rs.at[j - 1, e, f], (quad[f], h)
        ).wait_recv()

    for e in range(2):
        for j in range(1, ny):
            wx_copy(j, e).start()

    def x_copy(p, j):
        return remote(
            x_out.at[p], x_in.at[p, j - 1], x_ss.at[p, j - 1], x_rs.at[p, j - 1],
            (z * nx + lax.rem(x + j, nx), h),
        )

    def z_copy(p):
        return remote(
            z_out.at[p], z_in.at[p], z_ss.at[p], z_rs.at[p], (lax.rem(s + nx, n_seq), h)
        )

    stage = [0] * pairs

    def scan_one(p):
        n = stage[p]
        two = slice(2 * p, 2 * p + 2)
        if n == 0:
            x_out[p] = total[two].astype(BF16)
            for j in range(1, nx):
                x_copy(p, j).start()
        elif n == 1:
            whole = total[two]
            before = jnp.zeros_like(whole)
            for j in range(1, nx):
                x_copy(p, j).wait_recv()
                other = x_in[p, j - 1].astype(F32)
                whole = whole + other
                before = before + jnp.where(lax.rem(x - j + nx, nx) < x, other, 0.0)
            carried[two] = before
            group[two] = whole

            @pl.when(z == 0)
            def _():
                z_out[p] = whole.astype(BF16)
                z_copy(p).start()
        elif n <= nz:
            @pl.when(z == n - 1)
            def _():
                z_copy(p).wait_recv()
                got = z_in[p].astype(F32)
                carried[two] += got
                if n < nz:
                    z_out[p] = (got + group[two]).astype(BF16)
                    z_copy(p).start()
        else:
            return
        stage[p] = n + 1

    def scan_step(done):
        for p in range(done):
            scan_one(p)

    def project(w, dst, p, wait):
        @pl.loop(0, nu)
        def _(i):
            if wait:
                for j in range(ROWS // CHUNK):
                    tok_copy(i * (ROWS // CHUNK) + j).wait()
            rows = pl.ds(pl.multiple_of(i * ROWS, ROWS), ROWS)
            dst[rows, p * PAIR:(p + 1) * PAIR] = jnp.dot(
                tok[rows, :], w[...], preferred_element_type=F32
            ).astype(BF16)

    def piece(p, u):
        return pl.ds(u * ROWS, ROWS), pl.ds(p * PAIR, PAIR)

    def as_copy(p, u, head):
        r, l = piece(p, u)
        ref = att.at[head, r, l]
        return remote(ref, ref, as_ss.at[p, u], as_rs.at[p, u], (s, sib))

    def ay_copy(p, u, j, head):
        r, l = piece(p, u)
        ref = att.at[head, r, l]
        return remote(
            ref, ref, ay_ss.at[p, u, j - 1], ay_rs.at[p, u, j - 1],
            (s, lax.rem(y + j, ny) * 2 + c),
        )

    def af_copy(p, u, j, head):
        r, l = piece(p, u)
        ref = att.at[head, r, l]
        return remote(
            ref, ref, af_ss.at[p, u, j - 1], af_rs.at[p, u, j - 1], (s, sib)
        )

    def attention(p):
        keep = lax.broadcasted_iota(jnp.int32, (CHUNK, CHUNK), 0) >= lax.broadcasted_iota(
            jnp.int32, (CHUNK, CHUNK), 1
        )
        for u in range(nu):
            @pl.loop(u * (ROWS // CHUNK), (u + 1) * (ROWS // CHUNK))
            def _(t):
                rows = pl.ds(pl.multiple_of(t * CHUNK, CHUNK), CHUNK)
                for hd in (2 * p, 2 * p + 1):
                    lanes = slice(hd * HEAD_DIM, (hd + 1) * HEAD_DIM)
                    qh, kh, vh = q[rows, lanes], k[rows, lanes], v[rows, lanes]
                    scores = lax.dot_general(
                        qh, kh, (((1,), (1,)), ((), ())), preferred_element_type=F32
                    )
                    scores = jnp.where(keep, scores, 0.0).astype(BF16)
                    prior = (carried[hd] + pre[t, hd]).astype(BF16)
                    raw = jnp.dot(scores, vh, preferred_element_type=F32) + jnp.dot(
                        qh, prior, preferred_element_type=F32
                    )
                    power = jnp.mean(raw * raw, axis=-1, keepdims=True)
                    att[h, rows, lanes] = (
                        raw * lax.rsqrt(power + 1e-6) * gain_ref[:, lanes]
                    ).astype(BF16)

            for j in range(1, ny):
                ay_copy(p, u, j, h).start()
            as_copy(p, u, h).start()

    def forward(p):
        for u in range(nu):
            for j in range(1, ny):
                head = source(j, c)
                ay_copy(p, u, j, head).wait_recv()
                af_copy(p, u, j, head).start()

    for p in range(pairs):
        panel(wk_hbm, kbuf, k_sem, p).wait()
        if p == 0:
            panel(wq_hbm, qbuf, q_sem, 0).start()
        if p + 1 < pairs:
            panel(wk_hbm, kbuf, k_sem, p + 1).start()
        project(kbuf.at[p % 2], k, p, p == 0)
        scan_step(p)
        panel(wv_hbm, vbuf, v_sem, p).wait()
        if p + 1 < pairs:
            panel(wv_hbm, vbuf, v_sem, p + 1).start()
        project(vbuf.at[p % 2], v, p, False)
        for hd in (2 * p, 2 * p + 1):
            lanes = slice(hd * HEAD_DIM, (hd + 1) * HEAD_DIM)
            run = jnp.zeros((HEAD_DIM, HEAD_DIM), F32)
            for t in range(nt):
                pre[t, hd] = run
                run = run + lax.dot_general(
                    k[t * CHUNK:(t + 1) * CHUNK, lanes], v[t * CHUNK:(t + 1) * CHUNK, lanes],
                    (((0,), (0,)), ((), ())), preferred_element_type=F32,
                )
            total[hd] = run
        scan_step(p + 1)
        panel(wq_hbm, qbuf, q_sem, p).wait()
        if p + 1 < pairs:
            panel(wq_hbm, qbuf, q_sem, p + 1).start()
        if p == 0:
            own_copy.start()
            ws_copy().start()
        project(qbuf.at[p % 2], q, p, False)
        scan_step(p + 1)
        if p > 0:
            while stage[p - 1] <= nz:
                scan_one(p - 1)
            attention(p - 1)
        if p == 1:
            for e in range(2):
                for j in range(1, ny):
                    wx_wait(j, e)
                    for f in range(3):
                        wf_copy(j, e, f).start()

    last = pairs - 1
    scan_step(pairs)
    own_copy.wait()
    ws_wait()

    def add(t, head, lanes, first):
        rows = pl.ds(pl.multiple_of(t * CHUNK, CHUNK), CHUNK)
        term = jnp.dot(att[head, rows, lanes], wcol[head, lanes, :], preferred_element_type=F32)
        acc[rows, :] = term if first else acc[rows, :] + term

    ready = last * PAIR

    def add_all(head, lanes, first):
        @pl.loop(0, nt)
        def _(t):
            add(t, head, lanes, first)

    add_all(h, slice(0, ready), True)
    scan_step(pairs)
    if pairs > 1:
        forward(0)
    for p in range(last):
        for u in range(nu):
            as_copy(p, u, sib).wait_recv()
    while stage[last] <= nz:
        scan_one(last)
    attention(last)
    add_all(sib, slice(0, ready), False)
    for p in range(1, last):
        if p == 1:
            forward(p)
    add_all(h, slice(ready, width), False)
    for u in range(nu):
        as_copy(last, u, sib).wait_recv()
    add_all(sib, slice(ready, width), False)
    for e in range(2):
        for j in range(1, ny):
            for f in range(3):
                wf_wait(j, e, f)

    def out_copy(t):
        rows = pl.ds(t * CHUNK, CHUNK)
        return pltpu.make_async_copy(obuf.at[t], out_hbm.at[rows], o_sem.at[t])

    for p in range(pairs):
        lanes = slice(p * PAIR, (p + 1) * PAIR)
        for u in range(nu):
            if p >= 2 or p == last:
                for j in range(1, ny):
                    head = source(j, c)
                    ay_copy(p, u, j, head).wait_recv()
                    af_copy(p, u, j, head).start()
            for e in range(2):
                for j in range(1, ny):
                    if e == 0:
                        head = source(j, c)
                    else:
                        head = source(j, 1 - c)
                        af_copy(p, u, j, head).wait_recv()

                    @pl.loop(u * (ROWS // CHUNK), (u + 1) * (ROWS // CHUNK))
                    def _(t):
                        add(t, head, lanes, False)

            if p == last:
                for t in range(u * (ROWS // CHUNK), (u + 1) * (ROWS // CHUNK)):
                    obuf[t] = acc[t * CHUNK:(t + 1) * CHUNK, :].astype(BF16)
                    out_copy(t).start()

    for t in range(nt):
        out_copy(t).wait()
    ws_copy().wait_send()
    for e in range(2):
        for j in range(1, ny):
            wx_copy(j, e).wait_send()
            for f in range(3):
                wf_copy(j, e, f).wait_send()
    for p in range(pairs):
        for j in range(1, nx):
            x_copy(p, j).wait_send()

        @pl.when(z < nz - 1)
        def _():
            z_copy(p).wait_send()

        for u in range(nu):
            as_copy(p, u, h).wait_send()
            for j in range(1, ny):
                ay_copy(p, u, j, h).wait_send()
                af_copy(p, u, j, source(j, c)).wait_send()


def local(n_seq, n_head, nx, tokens, w_query, w_key, w_value, norm_gain, w_out):
    count, depth = tokens.shape
    width = w_query.shape[1]
    heads, pairs = width // HEAD_DIM, width // PAIR
    cols = w_out.shape[1] // n_head
    nt, nu, ny = count // CHUNK, count // ROWS, n_head // 2
    dma = pltpu.SemaphoreType.DMA
    hbm = pl.BlockSpec(memory_space=pl.ANY)
    vmem = pl.BlockSpec(memory_space=pltpu.VMEM)
    state = (HEAD_DIM, HEAD_DIM)
    return pl.pallas_call(
        functools.partial(kernel, n_seq, n_head, nx),
        out_shape=jax.ShapeDtypeStruct((count, cols), BF16),
        in_specs=[hbm, hbm, hbm, hbm, vmem, hbm],
        out_specs=hbm,
        scratch_shapes=[
            pltpu.VMEM((count, depth), BF16),
            pltpu.VMEM((2, depth, PAIR), BF16),
            pltpu.VMEM((2, depth, PAIR), BF16),
            pltpu.VMEM((2, depth, PAIR), BF16),
            pltpu.VMEM((count, width), BF16),
            pltpu.VMEM((count, width), BF16),
            pltpu.VMEM((count, width), BF16),
            pltpu.VMEM((n_head, count, width), BF16),
            pltpu.VMEM((n_head, width, cols), BF16),
            pltpu.VMEM((count, cols), F32),
            pltpu.VMEM((nt, heads, *state), F32),
            pltpu.VMEM((heads, *state), F32),
            pltpu.VMEM((heads, *state), F32),
            pltpu.VMEM((heads, *state), F32),
            pltpu.VMEM((pairs, 2, *state), BF16),
            pltpu.VMEM((pairs, nx - 1, 2, *state), BF16),
            pltpu.VMEM((pairs, 2, *state), BF16),
            pltpu.VMEM((pairs, 2, *state), BF16),
            pltpu.VMEM((nt, CHUNK, cols), BF16),
            dma((nt,)), dma((2,)), dma((2,)), dma((2,)), dma, dma((nt,)),
            dma((pairs, nx - 1)), dma((pairs, nx - 1)), dma((pairs,)), dma((pairs,)),
            dma, dma, dma((ny - 1, 2)), dma((ny - 1, 2)),
            dma((ny - 1, 2, 3)), dma((ny - 1, 2, 3)),
            dma((pairs, nu)), dma((pairs, nu)),
            dma((pairs, nu, ny - 1)), dma((pairs, nu, ny - 1)),
            dma((pairs, nu, ny - 1)), dma((pairs, nu, ny - 1)),
        ],
        compiler_params=pltpu.CompilerParams(
            collective_id=0, has_side_effects=True, vmem_limit_bytes=63 * 2**20
        ),
    )(tokens, w_query, w_key, w_value, norm_gain.reshape(1, width), w_out)


def solution(mesh):
    n_seq, n_head = mesh.shape["seq"], mesh.shape["head"]
    nx = 1 << ((n_seq.bit_length() - 1) // 2)
    in_specs = (
        P("seq", None), P(None, "head"), P(None, "head"), P(None, "head"),
        P("head"), P("head", None),
    )
    return jax.shard_map(
        functools.partial(local, n_seq, n_head, nx), mesh=mesh, in_specs=in_specs,
        out_specs=P("seq", "head"), check_vma=False,
    )
```

```python
import functools

import jax
import jax.numpy as jnp
from jax import lax
from jax.experimental import pallas as pl
from jax.experimental.pallas import tpu as pltpu
from jax.sharding import PartitionSpec as P

HEAD_DIM = 128
CHUNK = 256
PAIR = 2 * HEAD_DIM
ROWS = 512
AHEAD = 2
MESH = pl.DeviceIdType.MESH
BF16 = jnp.bfloat16
F32 = jnp.float32


def kernel(
    n_seq, n_head, nx,
    tok_hbm, wq_hbm, wk_hbm, wv_hbm, gain_ref, wo_hbm, out_hbm,
    tok, kbuf, vbuf, wq, wo, q, k, v, att, pre, total, carried,
    group, x_out, x_in, z_out, z_in, sib_out, sib_in, y_out, y_in, own, obuf,
    tok_sem, k_sem, v_sem, wq_sem, wo_sem, o_sem,
    x_ss, x_rs, z_ss, z_rs, sib_ss, sib_rs, y_ss, y_rs,
):
    count, depth = tok.shape
    width = q.shape[1]
    heads = width // HEAD_DIM
    pairs = width // PAIR
    cols = wo.shape[1] // n_head
    nt = count // CHUNK
    ny = n_head // 2
    nz = n_seq // nx
    s = lax.axis_index("seq")
    h = lax.axis_index("head")
    y, c = h // 2, h % 2
    sib = y * 2 + 1 - c
    z, x = s // nx, s % nx

    def remote(src, dst, ss, rs, dev):
        return pltpu.make_async_remote_copy(
            src_ref=src, dst_ref=dst, send_sem=ss, recv_sem=rs,
            device_id=dev, device_id_type=MESH,
        )

    def tok_copy(t):
        rows = pl.ds(pl.multiple_of(t * CHUNK, CHUNK), CHUNK)
        return pltpu.make_async_copy(tok_hbm.at[rows], tok.at[rows], tok_sem.at[t])

    def panel(src, dst, sem, p):
        return pltpu.make_async_copy(
            src.at[:, pl.ds(p * PAIR, PAIR)], dst.at[p % 2], sem.at[p % 2]
        )

    wq_copy = pltpu.make_async_copy(wq_hbm, wq, wq_sem)
    wo_copy = pltpu.make_async_copy(wo_hbm, wo, wo_sem)

    panel(wk_hbm, kbuf, k_sem, 0).start()
    for t in range(nt):
        tok_copy(t).start()
    panel(wv_hbm, vbuf, v_sem, 0).start()

    barrier = pltpu.get_barrier_semaphore()
    expected = jnp.int32(ny)
    pl.semaphore_signal(barrier, inc=1, device_id=(s, sib), device_id_type=MESH)
    for j in range(1, ny):
        peer = lax.rem(y + j, ny) * 2 + c
        pl.semaphore_signal(barrier, inc=1, device_id=(s, peer), device_id_type=MESH)
    for j in range(1, nx):
        pl.semaphore_signal(
            barrier, inc=1, device_id=(z * nx + lax.rem(x + j, nx), h), device_id_type=MESH
        )

    @pl.when(z > 0)
    def _():
        pl.semaphore_signal(barrier, inc=1, device_id=(s - nx, h), device_id_type=MESH)

    @pl.when(z < nz - 1)
    def _():
        pl.semaphore_signal(barrier, inc=1, device_id=(s + nx, h), device_id_type=MESH)

    expected += nx - 1 + (z > 0).astype(jnp.int32) + (z < nz - 1).astype(jnp.int32)
    pl.semaphore_wait(barrier, expected)

    def x_copy(p, j):
        return remote(
            x_out.at[p], x_in.at[p, j - 1], x_ss.at[p, j - 1], x_rs.at[p, j - 1],
            (z * nx + lax.rem(x + j, nx), h),
        )

    def z_copy(p):
        return remote(
            z_out.at[p], z_in.at[p], z_ss.at[p], z_rs.at[p], (lax.rem(s + nx, n_seq), h)
        )

    stage = [0] * pairs

    def scan_one(p):
        n = stage[p]
        two = slice(2 * p, 2 * p + 2)
        if n == 0:
            x_out[p] = total[two].astype(BF16)
            for j in range(1, nx):
                x_copy(p, j).start()
        elif n == 1:
            whole = total[two]
            before = jnp.zeros_like(whole)
            for j in range(1, nx):
                x_copy(p, j).wait_recv()
                other = x_in[p, j - 1].astype(F32)
                whole = whole + other
                before = before + jnp.where(lax.rem(x - j + nx, nx) < x, other, 0.0)
            carried[two] = before
            group[two] = whole

            @pl.when(z == 0)
            def _():
                z_out[p] = whole.astype(BF16)
                z_copy(p).start()
        elif n <= nz:
            @pl.when(z == n - 1)
            def _():
                z_copy(p).wait_recv()
                got = z_in[p].astype(F32)
                carried[two] += got
                if n < nz:
                    z_out[p] = (got + group[two]).astype(BF16)
                    z_copy(p).start()
        else:
            return
        stage[p] = n + 1

    def scan_step(done):
        for p in range(done):
            scan_one(p)

    def project(w, dst, p, wait):
        @pl.loop(0, count // ROWS)
        def _(i):
            if wait:
                for j in range(ROWS // CHUNK):
                    tok_copy(i * (ROWS // CHUNK) + j).wait()
            rows = pl.ds(pl.multiple_of(i * ROWS, ROWS), ROWS)
            dst[rows, p * PAIR:(p + 1) * PAIR] = jnp.dot(
                tok[rows, :], w[...], preferred_element_type=F32
            ).astype(BF16)

    for p in range(pairs):
        panel(wk_hbm, kbuf, k_sem, p).wait()
        if p + 1 < pairs:
            panel(wk_hbm, kbuf, k_sem, p + 1).start()
            panel(wv_hbm, vbuf, v_sem, p + 1).start()
        if p == pairs - 2:
            wq_copy.start()
        if p == pairs - 1:
            wo_copy.start()
        project(kbuf.at[p % 2], k, p, p == 0)
        if p > 0:
            scan_step(p)
        panel(wv_hbm, vbuf, v_sem, p).wait()
        project(vbuf.at[p % 2], v, p, False)
        for e in range(2):
            hd = 2 * p + e
            lanes = slice(hd * HEAD_DIM, (hd + 1) * HEAD_DIM)
            run = jnp.zeros((HEAD_DIM, HEAD_DIM), F32)
            for t in range(nt):
                pre[t, hd] = run
                run = run + lax.dot_general(
                    k[t * CHUNK:(t + 1) * CHUNK, lanes], v[t * CHUNK:(t + 1) * CHUNK, lanes],
                    (((0,), (0,)), ((), ())), preferred_element_type=F32,
                )
            total[hd] = run
        scan_step(p + 1)

    def project_q(t):
        rows = pl.ds(pl.multiple_of(t * CHUNK, CHUNK), CHUNK)

        @pl.loop(0, pairs)
        def _(i):
            lanes = pl.ds(pl.multiple_of(i * PAIR, PAIR), PAIR)
            q[rows, lanes] = jnp.dot(
                tok[rows, :], wq[:, lanes], preferred_element_type=F32
            ).astype(BF16)

    wq_copy.wait()
    for t in range(AHEAD):
        project_q(t)
        scan_step(pairs)
    while min(stage) <= nz:
        scan_step(pairs)
    wo_copy.wait()

    def sib_copy(t, j):
        return pltpu.make_async_remote_copy(
            src_ref=sib_out.at[t % 2, j], dst_ref=sib_in.at[t, j],
            send_sem=sib_ss.at[t, j], recv_sem=sib_rs.at[t, j],
            device_id=(s, sib), device_id_type=MESH,
        )

    def y_copy(t, j):
        return pltpu.make_async_remote_copy(
            src_ref=y_out.at[t, j - 1], dst_ref=y_in.at[t, j - 1],
            send_sem=y_ss.at[t, j - 1], recv_sem=y_rs.at[t, j - 1],
            device_id=(s, lax.rem(y + j, ny) * 2 + c), device_id_type=MESH,
        )

    def partial(dest):
        lanes = pl.ds(pl.multiple_of(dest * cols, cols), cols)
        return jnp.dot(att[...], wo[:, lanes], preferred_element_type=F32)

    order = list(range(1, ny)) + [0]

    @pl.loop(0, nt)
    def _(t):
        rows = pl.ds(pl.multiple_of(t * CHUNK, CHUNK), CHUNK)
        keep = lax.broadcasted_iota(jnp.int32, (CHUNK, CHUNK), 0) >= lax.broadcasted_iota(
            jnp.int32, (CHUNK, CHUNK), 1
        )
        for hd in range(heads):
            lanes = slice(hd * HEAD_DIM, (hd + 1) * HEAD_DIM)
            qh, kh, vh = q[rows, lanes], k[rows, lanes], v[rows, lanes]
            scores = lax.dot_general(
                qh, kh, (((1,), (1,)), ((), ())), preferred_element_type=F32
            )
            scores = jnp.where(keep, scores, 0.0).astype(BF16)
            prior = (carried[hd] + pre[t, hd]).astype(BF16)
            raw = jnp.dot(scores, vh, preferred_element_type=F32) + jnp.dot(
                qh, prior, preferred_element_type=F32
            )
            power = jnp.mean(raw * raw, axis=-1, keepdims=True)
            att[:, lanes] = (raw * lax.rsqrt(power + 1e-6) * gain_ref[:, lanes]).astype(BF16)

        @pl.when(t >= 2)
        def _():
            for j in range(ny):
                sib_copy(t - 2, j).wait_send()

        for j in order:
            sib_out[t % 2, j] = partial(lax.rem(y + j, ny) * 2 + 1 - c).astype(BF16)
            sib_copy(t, j).start()
        own[rows, :] = partial(h)
        for j in range(1, ny):
            mine = partial(lax.rem(y + j, ny) * 2 + c)
            sib_copy(t, j).wait_recv()
            y_out[t, j - 1] = (mine + sib_in[t, j].astype(F32)).astype(BF16)
            y_copy(t, j).start()
        sib_copy(t, 0).wait_recv()
        own[rows, :] += sib_in[t, 0].astype(F32)

        @pl.when(t + AHEAD < nt)
        def _():
            project_q(t + AHEAD)

    def out_copy(t):
        rows = pl.ds(t * CHUNK, CHUNK)
        return pltpu.make_async_copy(obuf.at[t % 2], out_hbm.at[rows], o_sem.at[t % 2])

    for t in range(nt):
        if t >= 2:
            out_copy(t - 2).wait()
        result = own[t * CHUNK:(t + 1) * CHUNK, :]
        for j in range(1, ny):
            y_copy(t, j).wait_recv()
            result = result + y_in[t, j - 1].astype(F32)
        obuf[t % 2] = result.astype(BF16)
        out_copy(t).start()
    for t in range(max(nt - 2, 0), nt):
        out_copy(t).wait()
        for j in range(ny):
            sib_copy(t, j).wait_send()
    for t in range(nt):
        for j in range(1, ny):
            y_copy(t, j).wait_send()
    for p in range(pairs):
        for j in range(1, nx):
            x_copy(p, j).wait_send()

        @pl.when(z < nz - 1)
        def _():
            z_copy(p).wait_send()


def local(n_seq, n_head, nx, tokens, w_query, w_key, w_value, norm_gain, w_out):
    count, depth = tokens.shape
    width = w_query.shape[1]
    heads, pairs = width // HEAD_DIM, width // PAIR
    features = w_out.shape[1]
    cols = features // n_head
    nt, ny = count // CHUNK, n_head // 2
    dma = pltpu.SemaphoreType.DMA
    hbm = pl.BlockSpec(memory_space=pl.ANY)
    vmem = pl.BlockSpec(memory_space=pltpu.VMEM)
    return pl.pallas_call(
        functools.partial(kernel, n_seq, n_head, nx),
        out_shape=jax.ShapeDtypeStruct((count, cols), BF16),
        in_specs=[hbm, hbm, hbm, hbm, vmem, hbm],
        out_specs=hbm,
        scratch_shapes=[
            pltpu.VMEM((count, depth), BF16),
            pltpu.VMEM((2, depth, PAIR), BF16),
            pltpu.VMEM((2, depth, PAIR), BF16),
            pltpu.VMEM((depth, width), BF16),
            pltpu.VMEM((width, features), BF16),
            pltpu.VMEM((count, width), BF16),
            pltpu.VMEM((count, width), BF16),
            pltpu.VMEM((count, width), BF16),
            pltpu.VMEM((CHUNK, width), BF16),
            pltpu.VMEM((nt, heads, HEAD_DIM, HEAD_DIM), F32),
            pltpu.VMEM((heads, HEAD_DIM, HEAD_DIM), F32),
            pltpu.VMEM((heads, HEAD_DIM, HEAD_DIM), F32),
            pltpu.VMEM((heads, HEAD_DIM, HEAD_DIM), F32),
            pltpu.VMEM((pairs, 2, HEAD_DIM, HEAD_DIM), BF16),
            pltpu.VMEM((pairs, nx - 1, 2, HEAD_DIM, HEAD_DIM), BF16),
            pltpu.VMEM((pairs, 2, HEAD_DIM, HEAD_DIM), BF16),
            pltpu.VMEM((pairs, 2, HEAD_DIM, HEAD_DIM), BF16),
            pltpu.VMEM((2, ny, CHUNK, cols), BF16),
            pltpu.VMEM((nt, ny, CHUNK, cols), BF16),
            pltpu.VMEM((nt, ny - 1, CHUNK, cols), BF16),
            pltpu.VMEM((nt, ny - 1, CHUNK, cols), BF16),
            pltpu.VMEM((count, cols), F32),
            pltpu.VMEM((2, CHUNK, cols), BF16),
            dma((nt,)), dma((2,)), dma((2,)), dma, dma, dma((2,)),
            dma((pairs, nx - 1)), dma((pairs, nx - 1)), dma((pairs,)), dma((pairs,)),
            dma((nt, ny)), dma((nt, ny)),
            dma((nt, ny - 1)), dma((nt, ny - 1)),
        ],
        compiler_params=pltpu.CompilerParams(
            collective_id=0, has_side_effects=True, vmem_limit_bytes=63 * 2**20
        ),
    )(tokens, w_query, w_key, w_value, norm_gain.reshape(1, width), w_out)


def solution(mesh):
    n_seq, n_head = mesh.shape["seq"], mesh.shape["head"]
    nx = 1 << ((n_seq.bit_length() - 1) // 2)
    in_specs = (
        P("seq", None), P(None, "head"), P(None, "head"), P(None, "head"),
        P("head"), P("head", None),
    )
    return jax.shard_map(
        functools.partial(local, n_seq, n_head, nx), mesh=mesh, in_specs=in_specs,
        out_specs=P("seq", "head"), check_vma=False,
    )
```
